32 devices in a mesh: fsdp: 32 (over z, y, x, core).
Axes of the slice: x: 2, y: 2, z: 4, core: 2. Of those that a mesh axis runs over, the one named last changes fastest.
Arguments:
- tokens: bfloat16 [16384, 1024], P('fsdp'), may hold values from -6 to 6
- segment_ids: int32 [16384], P('fsdp'), may hold values from -1 to 3, as said below
- cotangent: bfloat16 [16384, 1024], P('fsdp'), may hold values from -6 to 6
- w_qkv: bfloat16 [1024, 3072], P('fsdp'), may hold values from -0.1875 to 0.1875
- w_out: bfloat16 [1024, 1024], P('fsdp'), may hold values from -0.75 to 0.75
- w_up: bfloat16 [1024, 4096], P('fsdp'), may hold values from -0.1875 to 0.1875
- w_down: bfloat16 [4096, 1024], P('fsdp'), may hold values from -0.09375 to 0.09375
- b_qkv: bfloat16 [3072], P('fsdp'), may hold values from -1.5 to 1.5
- b_out: bfloat16 [1024], P('fsdp'), may hold values from -1.5 to 1.5
- b_up: bfloat16 [4096], P('fsdp'), may hold values from -1.5 to 1.5
- b_down: bfloat16 [1024], P('fsdp'), may hold values from -1.5 to 1.5
- gain_attn: bfloat16 [1024], P('fsdp'), may hold values from 0.5 to 1.5
- shift_attn: bfloat16 [1024], P('fsdp'), may hold values from -1.5 to 1.5
- gain_mlp: bfloat16 [1024], P('fsdp'), may hold values from 0.5 to 1.5
- shift_mlp: bfloat16 [1024], P('fsdp'), may hold values from -1.5 to 1.5
Outputs:
- layer_out: bfloat16 [16384, 1024], P('fsdp')
- tokens_grad: float32 [16384, 1024], P('fsdp')
- grad_w_qkv: float32 [1024, 3072], P('fsdp')
- grad_w_out: float32 [1024, 1024], P('fsdp')
- grad_w_up: float32 [1024, 4096], P('fsdp')
- grad_w_down: float32 [4096, 1024], P('fsdp')
- grad_b_qkv: float32 [3072], P('fsdp')
- grad_b_out: float32 [1024], P('fsdp')
- grad_b_up: float32 [4096], P('fsdp')
- grad_b_down: float32 [1024], P('fsdp')
- grad_gain_attn: float32 [1024], P('fsdp')
- grad_shift_attn: float32 [1024], P('fsdp')
- grad_gain_mlp: float32 [1024], P('fsdp')
- grad_shift_mlp: float32 [1024], P('fsdp')
The draws below stay inside these ranges and needn't reach their ends.
Inputs may be any that keep to these rules, and one draw needn't show every extreme that they name: `segment_ids`: each device's 512 slots form blocks of 128; a sequence starts at a block's first slot and covers whole consecutive blocks of one device; its live slots are a prefix and the rest of its last block is padding marked -1; live slots carry the sequence's number on its device, counted from 0 in order of slots.
All inputs are finite; a program needn't handle non-finite values.
Results may differ from the reference program's by a relative error of at most 0.0095.
Values may be sent and summed in bfloat16 or wider, within the bound.
No kernel may reach another device: no remote copies, remote signals or barrier semaphores. Data moves between devices by JAX's collectives and lax.ppermute only.
A program may use at most 256 MiB of HBM per device.

```python
import jax
import jax.numpy as jnp
from jax import lax

D = 1024
FF = 4096
HEADS = 16
HEAD_DIM = 64
ROTARY = 16
BLOCK = 128
TOK_DEV = 512
TOKENS = 16384
N_FSDP = 32


def draw_segment_ids(key, part):
    key = jax.random.fold_in(key, 7)
    subkeys = jax.random.split(key, 5)
    devices = TOKENS // TOK_DEV
    blocks = TOK_DEV // BLOCK
    starts = jax.random.randint(subkeys[0], (devices, blocks), 0, 2)
    device_index = jnp.arange(devices)[:, None]
    block_index = jnp.arange(blocks)[None, :]
    starts = jnp.where(block_index == 0, 1, starts)
    chosen = jax.random.randint(subkeys[1], (), 0, devices)
    second_device = (chosen + 1 + jax.random.randint(subkeys[2], (), 0, devices - 1)) % devices
    starts = jnp.where(device_index == chosen, 1, starts)
    starts = jnp.where((device_index == second_device) & (block_index > 0), 0, starts)
    numbers = jnp.cumsum(starts, axis=1) - 1
    following = jnp.concatenate([starts[:, 1:], jnp.ones((devices, 1), starts.dtype)], axis=1)
    live_count = jax.random.randint(subkeys[3], (devices, blocks), 1, BLOCK + 1)
    short_count = jax.random.randint(subkeys[4], (devices, blocks), 1, BLOCK)
    live_count = jnp.where(device_index == chosen, short_count, live_count)
    live_count = jnp.where(following == 1, live_count, BLOCK)
    slot_index = jnp.arange(BLOCK)[None, None, :]
    segment = jnp.where(slot_index < live_count[:, :, None], numbers[:, :, None], -1)
    return segment.reshape(TOKENS).astype(jnp.int32)


def strengthened(entries, stream_key, source, target, blocks, factor):
    owner, partner = [(jnp.arange(entries.shape[axis_at]) // (entries.shape[axis_at] // blocks)).reshape([-1 if axis == axis_at else 1 for axis in range(entries.ndim)]) for axis_at in (source, target)]
    chosen = jax.random.permutation(stream_key, blocks)[partner]
    strong = (owner == chosen) | (owner == (partner + blocks // 2) % blocks)
    return jnp.where(strong, factor * entries, entries)


def levels(rng, extent, cuts, smallest, high):
    def one(dim, blocks):
        heights = jax.random.uniform(jax.random.fold_in(jax.random.fold_in(rng, 6), dim), (blocks,), jnp.float32, smallest / len(cuts), high / len(cuts))
        return jnp.repeat(jnp.exp(heights), extent[dim] // blocks).reshape((-1,) + (1,) * (len(extent) - dim - 1))

    level = one(*cuts[0])
    for cut in cuts[1:]:
        level = level * one(*cut)
    return level


def scatter_about(own_key, shape, scale, reach, cuts=(), kind=jnp.bfloat16):
    entries = jax.random.normal(own_key, shape, jnp.float32) * scale
    if len(cuts) > 0:
        entries = levels(own_key, shape, cuts, -0.22, 0.18) * entries
    return jnp.clip(entries, min=-reach, max=reach).astype(kind)


def noise_with(own_key, extent, scale, bound, cuts, heavy, held_as=jnp.bfloat16):
    values = scale * jax.random.normal(own_key, extent, jnp.float32)
    if cuts:
        values = values * levels(own_key, extent, cuts, -0.22, 0.18)
    return jnp.clip(strengthened(values, jax.random.fold_in(own_key, 3), *heavy), -bound, bound).astype(held_as)


def setup_inputs(seed: int = 0) -> dict:
    splits = jax.random.split(jax.random.key(seed), 16)
    return {
        "tokens": scatter_about(splits[0], (TOKENS, D), 1.0, 6.0, ((0, 32),)),
        "segment_ids": draw_segment_ids(jax.random.fold_in(splits[15], 71), 0),
        "cotangent": noise_with(splits[2], (TOKENS, D), 1.0, 6.0, ((0, 32),), (0, 1, 32, 2.75)),
        "w_qkv": scatter_about(splits[3], (D, 3 * D), D ** -0.5, 0.1875, ((0, 32),)),
        "w_out": scatter_about(splits[4], (D, D), (D // 16) ** -0.5, 0.75, ((0, 32),)),
        "w_up": scatter_about(splits[5], (D, FF), D ** -0.5, 0.1875, ((0, 32),)),
        "w_down": scatter_about(splits[6], (FF, D), FF ** -0.5, 0.09375, ((0, 32),)),
        "b_qkv": scatter_about(splits[7], (3 * D,), 0.3, 1.5, ((0, 32),)),
        "b_out": scatter_about(splits[8], (D,), 0.3, 1.5, ((0, 32),)),
        "b_up": scatter_about(splits[9], (FF,), 0.3, 1.5, ((0, 32),)),
        "b_down": scatter_about(splits[10], (D,), 0.3, 1.5, ((0, 32),)),
        "gain_attn": jnp.clip(1.0 + 0.1 * jax.random.normal(splits[11], (D,), jnp.float32), 0.5, 1.5).astype(jnp.bfloat16),
        "shift_attn": scatter_about(splits[12], (D,), 0.3, 1.5, ((0, 32),)),
        "gain_mlp": jnp.clip(1.0 + 0.1 * jax.random.normal(splits[13], (D,), jnp.float32), 0.5, 1.5).astype(jnp.bfloat16),
        "shift_mlp": scatter_about(splits[14], (D,), 0.3, 1.5, ((0, 32),)),
    }


epsilon = 1e-05
highest = lax.Precision.HIGHEST

@jax.custom_vjp
def low(v):
    return lax.optimization_barrier(v.astype(jnp.bfloat16)).astype(jnp.float32)

@jax.custom_vjp
def low_back(v):
    return v

def low_keep(v):
    return (low(v), None)

def low_pass(kept, grad):
    return (grad,)

def back_keep(v):
    return (v, None)

def back_low(kept, grad):
    return (low(grad),)
low.defvjp(low_keep, low_pass)
low_back.defvjp(back_keep, back_low)

def matmul(left_side, right_side):
    return jnp.dot(left_side, right_side, precision=highest)

def layer_norm(inputs, gain, shift):
    center = inputs - lax.optimization_barrier(jnp.mean(inputs, axis=-1, keepdims=True))
    scaled = center * lax.rsqrt(lax.optimization_barrier(jnp.mean(center * center, axis=-1, keepdims=True)) + epsilon)
    return scaled * gain + shift

def rotary_tables(position):
    inv_freq = 10000.0 ** (-jnp.arange(ROTARY // 2, dtype=jnp.float32) * 2.0 / ROTARY)
    angles = position[:, None] * inv_freq[None, :]
    return (jnp.cos(angles)[:, None, :], jnp.sin(angles)[:, None, :])

def rotate(features, cos_table, sin_table):
    half_dims = ROTARY // 2
    lower_half = features[..., :half_dims]
    upper_half = features[..., half_dims:ROTARY]
    return jnp.concatenate([lower_half * cos_table - upper_half * sin_table, upper_half * cos_table + lower_half * sin_table, features[..., ROTARY:]], axis=-1)

def device_positions(segment):
    tok_count = segment.shape[0]
    tok_index = jnp.arange(tok_count, dtype=jnp.int32)
    same_seq = segment[:, None] == segment[None, :]
    seq_start = lax.optimization_barrier(jnp.min(jnp.where(same_seq, tok_index[None, :], tok_count), axis=1))
    return (tok_index - seq_start).astype(jnp.float32)

def allowed_mask(seg_rows, seg_cols, row_index, col_index):
    same_seq = (seg_rows[:, None] == seg_cols[None, :]) & (seg_cols[None, :] >= 0) & (col_index[None, :] <= row_index[:, None])
    return same_seq | (col_index[None, :] == row_index[:, None])

def attend_device(operands):
    query_rot, key_rot, value_low, segment = operands
    tok_index = jnp.arange(segment.shape[0], dtype=jnp.int32)
    allowed = allowed_mask(segment, segment, tok_index, tok_index)
    scores = low_back(jnp.einsum('qhd,khd->hqk', query_rot, key_rot, precision=highest) * HEAD_DIM ** (-0.5))
    scores = jnp.where(allowed[None], scores, -1e+30)
    row_max = lax.optimization_barrier(jnp.max(scores, axis=-1, keepdims=True))
    weights = jnp.exp(scores - row_max)
    attn_prob = low(weights / lax.optimization_barrier(jnp.sum(weights, axis=-1, keepdims=True)))
    return jnp.einsum('hqk,khd->qhd', attn_prob, value_low, precision=highest)

def reference(tokens, segment_ids, cotangent, w_qkv, w_out, w_up, w_down, b_qkv, b_out, b_up, b_down, gain_attn, shift_attn, gain_mlp, shift_mlp):
    segment_dev = segment_ids.reshape(N_FSDP, TOK_DEV)
    position = lax.map(device_positions, segment_dev).reshape(TOKENS)
    cos_table, sin_table = rotary_tables(position)

    def forward(inputs, weight_qkv, weight_out, weight_up, weight_down, bias_qkv, bias_out, bias_up, bias_down, gain_one, shift_one, gain_two, shift_two):
        normed_attn = low(layer_norm(inputs, gain_one, shift_one))
        normed_mlp = low(layer_norm(inputs, gain_two, shift_two))
        joined = low_back(matmul(normed_attn, weight_qkv) + bias_qkv)
        query_rot = low(rotate(joined[:, :D].reshape(TOKENS, HEADS, HEAD_DIM), cos_table, sin_table))
        key_rot = low(rotate(joined[:, D:2 * D].reshape(TOKENS, HEADS, HEAD_DIM), cos_table, sin_table))
        value_low = low(joined[:, 2 * D:].reshape(TOKENS, HEADS, HEAD_DIM))
        mixed = lax.map(jax.checkpoint(attend_device), (query_rot.reshape(N_FSDP, TOK_DEV, HEADS, HEAD_DIM), key_rot.reshape(N_FSDP, TOK_DEV, HEADS, HEAD_DIM), value_low.reshape(N_FSDP, TOK_DEV, HEADS, HEAD_DIM), segment_dev))
        attended = low(low_back(mixed.reshape(TOKENS, D)))
        branch_attn = low_back(matmul(attended, weight_out) + bias_out)
        pre_up = low_back(matmul(normed_mlp, weight_up) + bias_up)
        hidden = low(jax.nn.gelu(pre_up, approximate=False))
        branch_mlp = low_back(matmul(hidden, weight_down) + bias_down)
        return inputs + branch_attn + branch_mlp
    primals = [weight.astype(jnp.float32) for weight in (tokens, w_qkv, w_out, w_up, w_down, b_qkv, b_out, b_up, b_down, gain_attn, shift_attn, gain_mlp, shift_mlp)]
    outputs, pullback = jax.vjp(forward, *primals)
    live_rows = (segment_ids >= 0).astype(jnp.float32)
    grads = pullback(cotangent.astype(jnp.float32) * live_rows[:, None])
    return (outputs.astype(jnp.bfloat16), grads[0], grads[1], grads[2], grads[3], grads[4], grads[5], grads[6], grads[7], grads[8], grads[9], grads[10], grads[11], grads[12])
```

```python
from functools import partial

import jax
import jax.numpy as jnp
from jax import lax
from jax.experimental import pallas as pl
from jax.experimental.pallas import tpu as pltpu
from jax.sharding import PartitionSpec as P

D = 1024
HEADS = 16
HEAD_DIM = 64
ROTARY = 16


epsilon = 1e-05


def rotary_tables(position):
    inv_freq = 10000.0 ** (-jnp.arange(ROTARY // 2, dtype=jnp.float32) * 2.0 / ROTARY)
    angles = position[:, None] * inv_freq[None, :]
    return (jnp.cos(angles)[:, None, :], jnp.sin(angles)[:, None, :])


def rotate(features, cos_table, sin_table):
    half_dims = ROTARY // 2
    lower_half = features[..., :half_dims]
    upper_half = features[..., half_dims:ROTARY]
    return jnp.concatenate(
        [
            lower_half * cos_table - upper_half * sin_table,
            upper_half * cos_table + lower_half * sin_table,
            features[..., ROTARY:],
        ],
        axis=-1,
    )


def allowed_mask(seg_rows, seg_cols, row_index, col_index):
    same_seq = (
        (seg_rows[:, None] == seg_cols[None, :])
        & (seg_cols[None, :] >= 0)
        & (col_index[None, :] <= row_index[:, None])
    )
    return same_seq | (col_index[None, :] == row_index[:, None])


def inner_rows(left_side, right_side):
    return lax.dot_general(
        left_side, right_side, (((0,), (0,)), ((), ())), preferred_element_type=jnp.float32
    )


def times_transpose(left_side, right_side):
    return lax.dot_general(
        left_side, right_side, (((1,), (1,)), ((), ())), preferred_element_type=jnp.float32
    )


def block_scores(query_block, key_part, segment_ids, tok_index):
    raw_scores = jnp.einsum(
        "qhd,khd->hqk", query_block, key_part, preferred_element_type=jnp.float32
    ) * HEAD_DIM ** (-0.5)
    allowed = allowed_mask(segment_ids, segment_ids, tok_index, tok_index)
    return jnp.where(allowed[None], raw_scores, -1e30)


def column_sums(values):
    return jnp.sum(values.astype(jnp.float32), axis=0)


def on_device_any(
    tokens,
    segment_ids,
    cotangent,
    w_qkv,
    w_out,
    w_up,
    w_down,
    b_qkv,
    b_out,
    b_up,
    b_down,
    gain_attn,
    shift_attn,
    gain_mlp,
    shift_mlp,
):
    gathered = (
        lax.all_gather(w_qkv, "fsdp", axis=0, tiled=True),
        lax.all_gather(w_out, "fsdp", axis=0, tiled=True),
        lax.all_gather(w_up, "fsdp", axis=0, tiled=True),
        lax.all_gather(w_down, "fsdp", axis=0, tiled=True),
        lax.all_gather(b_qkv, "fsdp", axis=0, tiled=True),
        lax.all_gather(b_out, "fsdp", axis=0, tiled=True),
        lax.all_gather(b_up, "fsdp", axis=0, tiled=True),
        lax.all_gather(b_down, "fsdp", axis=0, tiled=True),
        lax.all_gather(gain_attn, "fsdp", axis=0, tiled=True),
        lax.all_gather(shift_attn, "fsdp", axis=0, tiled=True),
        lax.all_gather(gain_mlp, "fsdp", axis=0, tiled=True),
        lax.all_gather(shift_mlp, "fsdp", axis=0, tiled=True),
    )
    wqkv_all, wout_all, wup_all, wdown_all = (gathered[0], gathered[1], gathered[2], gathered[3])
    bias_qkv = gathered[4].astype(jnp.float32)
    bias_out = gathered[5].astype(jnp.float32)
    bias_up = gathered[6].astype(jnp.float32)
    bias_down = gathered[7].astype(jnp.float32)
    gain_one = gathered[8].astype(jnp.float32)
    shift_one = gathered[9].astype(jnp.float32)
    gain_two = gathered[10].astype(jnp.float32)
    shift_two = gathered[11].astype(jnp.float32)
    tok_count = tokens.shape[0]
    tok_index = jnp.arange(tok_count, dtype=jnp.int32)
    same_seq = segment_ids[:, None] == segment_ids[None, :]
    seq_start = jnp.min(jnp.where(same_seq, tok_index[None, :], tok_count), axis=1)
    position = (tok_index - seq_start).astype(jnp.float32)
    cos_table, sin_table = rotary_tables(position)
    inputs = tokens.astype(jnp.float32)
    center = inputs - jnp.mean(inputs, axis=-1, keepdims=True)
    inv_scale = lax.rsqrt(jnp.mean(center * center, axis=-1, keepdims=True) + epsilon)
    normed = center * inv_scale
    h_attn = (normed * gain_one + shift_one).astype(jnp.bfloat16)
    h_mlp = (normed * gain_two + shift_two).astype(jnp.bfloat16)
    joined = jnp.dot(h_attn, wqkv_all, preferred_element_type=jnp.float32) + bias_qkv
    query_rot = rotate(
        joined[:, :D].reshape(tok_count, HEADS, HEAD_DIM), cos_table, sin_table
    ).astype(jnp.bfloat16)
    key_rot = rotate(
        joined[:, D : 2 * D].reshape(tok_count, HEADS, HEAD_DIM), cos_table, sin_table
    ).astype(jnp.bfloat16)
    value_low = joined[:, 2 * D :].reshape(tok_count, HEADS, HEAD_DIM).astype(jnp.bfloat16)
    block_rows = min(512, tok_count)
    scores = block_scores(query_rot, key_rot, segment_ids, tok_index)
    row_max = jnp.max(scores, axis=-1, keepdims=True)
    weights = jnp.exp(scores - row_max)
    row_sum = jnp.sum(weights, axis=-1, keepdims=True)
    attn_prob = (weights / row_sum).astype(jnp.bfloat16)
    attended_blocks = jnp.einsum(
        "hqk,khd->qhd", attn_prob, value_low, preferred_element_type=jnp.float32
    )
    attended = attended_blocks.reshape(tok_count, D).astype(jnp.bfloat16)
    branch_attn = jnp.dot(attended, wout_all, preferred_element_type=jnp.float32) + bias_out
    pre_up = jnp.dot(h_mlp, wup_all, preferred_element_type=jnp.float32) + bias_up
    gelu_value, gelu_pull = jax.vjp(partial(jax.nn.gelu, approximate=False), pre_up)
    hidden = gelu_value.astype(jnp.bfloat16)
    branch_mlp = jnp.dot(hidden, wdown_all, preferred_element_type=jnp.float32) + bias_down
    layer_out = (inputs + branch_attn + branch_mlp).astype(jnp.bfloat16)
    again = (
        lax.all_gather(w_qkv, "fsdp", axis=0, tiled=True),
        lax.all_gather(w_out, "fsdp", axis=0, tiled=True),
        lax.all_gather(w_up, "fsdp", axis=0, tiled=True),
        lax.all_gather(w_down, "fsdp", axis=0, tiled=True),
        lax.all_gather(gain_attn, "fsdp", axis=0, tiled=True),
        lax.all_gather(gain_mlp, "fsdp", axis=0, tiled=True),
    )
    wqkv_bwd, wout_bwd, wup_bwd, wdown_bwd = (again[0], again[1], again[2], again[3])
    gain_one_bwd = again[4].astype(jnp.float32)
    gain_two_bwd = again[5].astype(jnp.float32)
    live_rows = (segment_ids >= 0).astype(jnp.float32)
    grad_out = cotangent.astype(jnp.float32) * live_rows[:, None]
    grad_low = grad_out.astype(jnp.bfloat16)
    grad_bias_out = column_sums(grad_low)
    grad_wout = inner_rows(attended, grad_low)
    grad_wdown = inner_rows(hidden, grad_low)
    d_hidden = times_transpose(grad_low, wdown_bwd)
    d_pre = gelu_pull(d_hidden)[0].astype(jnp.bfloat16)
    grad_bias_up = column_sums(d_pre)
    grad_wup = inner_rows(h_mlp, d_pre)
    d_h_mlp = times_transpose(d_pre, wup_bwd)
    grad_gain_mlp = jnp.sum(d_h_mlp * normed, axis=0)
    grad_shift_mlp = jnp.sum(d_h_mlp, axis=0)
    d_att = (
        times_transpose(grad_low, wout_bwd).astype(jnp.bfloat16).reshape(tok_count, HEADS, HEAD_DIM)
    )
    key_grad = jnp.zeros((tok_count, HEADS, HEAD_DIM), jnp.float32)
    value_grad = jnp.zeros((tok_count, HEADS, HEAD_DIM), jnp.float32)
    scores = block_scores(query_rot, key_rot, segment_ids, tok_index)
    attn_prob = jnp.exp(scores - row_max) / row_sum
    d_prob = jnp.einsum("qhd,khd->hqk", d_att, value_low, preferred_element_type=jnp.float32)
    row_dot = jnp.sum(attn_prob * d_prob, axis=-1, keepdims=True)
    d_score = (attn_prob * (d_prob - row_dot)).astype(jnp.bfloat16)
    query_grads = jnp.einsum(
        "hqk,khd->qhd", d_score, key_rot, preferred_element_type=jnp.float32
    ) * HEAD_DIM ** (-0.5)
    key_grad = key_grad.at[:block_rows].add(
        jnp.einsum("hqk,qhd->khd", d_score, query_rot, preferred_element_type=jnp.float32)
        * HEAD_DIM ** (-0.5)
    )
    value_grad = value_grad.at[:block_rows].add(
        jnp.einsum(
            "hqk,qhd->khd",
            attn_prob.astype(jnp.bfloat16),
            d_att,
            preferred_element_type=jnp.float32,
        )
    )
    query_grad = rotate(query_grads, cos_table, -sin_table)
    key_grad = rotate(key_grad, cos_table, -sin_table)
    d_joined = jnp.concatenate(
        [
            query_grad.reshape(tok_count, D),
            key_grad.reshape(tok_count, D),
            value_grad.reshape(tok_count, D),
        ],
        axis=1,
    ).astype(jnp.bfloat16)
    grad_bias_qkv = column_sums(d_joined)
    grad_wqkv = inner_rows(h_attn, d_joined)
    d_h_attn = times_transpose(d_joined, wqkv_bwd)
    grad_gain_attn = jnp.sum(d_h_attn * normed, axis=0)
    grad_shift_attn = jnp.sum(d_h_attn, axis=0)
    d_norm = d_h_attn * gain_one_bwd + d_h_mlp * gain_two_bwd
    d_inner = (
        d_norm
        - jnp.mean(d_norm, axis=-1, keepdims=True)
        - normed * jnp.mean(d_norm * normed, axis=-1, keepdims=True)
    )
    tokens_grad = grad_out + d_inner * inv_scale
    all_sums = (
        lax.psum_scatter(grad_wqkv, "fsdp", scatter_dimension=0, tiled=True),
        lax.psum_scatter(grad_wout, "fsdp", scatter_dimension=0, tiled=True),
        lax.psum_scatter(grad_wup, "fsdp", scatter_dimension=0, tiled=True),
        lax.psum_scatter(grad_wdown, "fsdp", scatter_dimension=0, tiled=True),
        lax.psum_scatter(grad_bias_qkv, "fsdp", scatter_dimension=0, tiled=True),
        lax.psum_scatter(grad_bias_out, "fsdp", scatter_dimension=0, tiled=True),
        lax.psum_scatter(grad_bias_up, "fsdp", scatter_dimension=0, tiled=True),
        lax.psum_scatter(grad_gain_attn, "fsdp", scatter_dimension=0, tiled=True),
        lax.psum_scatter(grad_shift_attn, "fsdp", scatter_dimension=0, tiled=True),
        lax.psum_scatter(grad_gain_mlp, "fsdp", scatter_dimension=0, tiled=True),
        lax.psum_scatter(grad_shift_mlp, "fsdp", scatter_dimension=0, tiled=True),
    )
    return (
        layer_out,
        tokens_grad,
        all_sums[0],
        all_sums[1],
        all_sums[2],
        all_sums[3],
        all_sums[4],
        all_sums[5],
        all_sums[6],
        all_sums[5],
        all_sums[7],
        all_sums[8],
        all_sums[9],
        all_sums[10],
    )


BF16 = jnp.bfloat16
F32 = jnp.float32
PLANE = 8
LINE = 4
DEVICES = PLANE * LINE
SLOTS = 512
HELD = PLANE * SLOTS
FF_PART = 512
QKV_PART = 384
VMEM_BYTES = 56 * 1024 * 1024


def exchange(values, partner):
    return lax.ppermute(values, "fsdp", [(i, partner(i)) for i in range(DEVICES)])


def swap_core(values):
    return exchange(values, lambda i: i ^ 1)


def swap_near(values):
    return exchange(values, lambda i: i ^ (4 if i % 2 else 2))


def swap_far(values):
    return exchange(values, lambda i: i ^ (2 if i % 2 else 4))


def over_groups(values, groups):
    return lax.all_to_all(
        values, "fsdp", split_axis=0, concat_axis=0, tiled=True, axis_index_groups=groups
    )


def over_plane(values):
    return over_groups(values, [[PLANE * z + r for r in range(PLANE)] for z in range(LINE)])


def over_line(values):
    return over_groups(values, [[PLANE * z + r for z in range(LINE)] for r in range(PLANE)])


def gather_line(values):
    return over_line(jnp.broadcast_to(values[None], (LINE,) + values.shape))


def sum_line(values):
    return jnp.sum(over_line(values).astype(F32), axis=0)


def spread_tokens(own):
    pair = jnp.concatenate([own, swap_near(own)])
    half = jnp.concatenate([pair, swap_far(pair)])
    return jnp.concatenate([half, swap_core(half)])


def add_low(left_side, right_side):
    return (left_side.astype(F32) + right_side.astype(F32)).astype(BF16)


def collect_tokens(part):
    half = add_low(part[: HELD // 2], swap_core(part[HELD // 2 :]))
    pair = add_low(half[: 2 * SLOTS], swap_far(half[2 * SLOTS :]))
    return pair[:SLOTS].astype(F32) + swap_near(pair[SLOTS:]).astype(F32)


def normalize(rows):
    center = rows - jnp.mean(rows, axis=-1, keepdims=True)
    inv_scale = lax.rsqrt(jnp.mean(center * center, axis=-1, keepdims=True) + epsilon)
    return (center * inv_scale, inv_scale)


def plain(left_side, right_side):
    return lax.dot_general(
        left_side, right_side, (((1,), (0,)), ((), ())), preferred_element_type=F32
    )


def swap_pairs(values):
    lane = lax.broadcasted_iota(jnp.int32, values.shape, 1)
    return jnp.where(
        (lane & 8) == 0, pltpu.roll(values, 120, axis=1), pltpu.roll(values, 8, axis=1)
    )


def up_kernel(tok_ref, w_ref, gain_ref, shift_ref, bias_ref, h_ref, hidden_ref, slope_ref):
    normed, _ = normalize(tok_ref[...].astype(F32))
    h_low = (normed * gain_ref[...] + shift_ref[...]).astype(BF16)
    h_ref[...] = h_low
    pre = plain(h_low, w_ref[...]) + bias_ref[...]
    cdf = 0.5 + 0.5 * lax.erf(pre * 0.5**0.5)
    hidden_ref[...] = (pre * cdf).astype(BF16)
    slope_ref[...] = cdf + pre * jnp.exp(-0.5 * pre * pre) * 0.3989422804014327


def qkv_kernel(tok_ref, w_ref, gain_ref, shift_ref, bias_ref, cos_ref, sin_ref, h_ref, qkv_ref):
    normed, _ = normalize(tok_ref[...].astype(F32))
    h_low = (normed * gain_ref[...] + shift_ref[...]).astype(BF16)
    h_ref[...] = h_low
    joined = plain(h_low, w_ref[...]) + bias_ref[...]
    cos_rows, sin_rows = cos_ref[...], sin_ref[...]
    for part in range(2):
        rows = joined[:, 128 * part : 128 * part + 128]
        qkv_ref[:, 128 * part : 128 * part + 128] = (
            rows * cos_rows + swap_pairs(rows) * sin_rows
        ).astype(BF16)
    qkv_ref[:, 256:] = joined[:, 256:].astype(BF16)


def accumulate(total_ref, step, value):
    @pl.when(step == 0)
    def _():
        total_ref[...] = value

    @pl.when(step > 0)
    def _():
        total_ref[...] += value


def down_kernel(
    grad_ref, h_ref, hidden_ref, slope_ref, w_down_ref, w_up_ref, gain_ref,
    branch_ref, dnorm_ref, dw_down_ref, dw_up_ref, db_ref, dot_ref, shift_ref,
    down_acc, up_acc,
):
    step = pl.program_id(0)
    grad, hidden = grad_ref[...], hidden_ref[...]
    w_down, w_up = w_down_ref[...], w_up_ref[...]
    d_pre = times_transpose(grad, w_down) * slope_ref[...]
    d_low = d_pre.astype(BF16)
    accumulate(db_ref, step, jnp.sum(d_low.astype(F32), axis=0, keepdims=True))
    branch_ref[...] = plain(hidden, w_down).astype(BF16)
    dnorm_ref[...] = (times_transpose(d_low, w_up) * gain_ref[...]).astype(BF16)
    accumulate(down_acc, step, inner_rows(hidden, grad))
    accumulate(up_acc, step, inner_rows(h_ref[...], d_low))

    @pl.when(step == pl.num_programs(0) - 1)
    def _():
        dw_down_ref[...] = down_acc[...].astype(BF16)
        dw_up_ref[...] = up_acc[...].astype(BF16)
        weights = w_up.astype(F32)
        dot_ref[...] = jnp.sum(weights * up_acc[...], axis=1, keepdims=True)
        shift_ref[...] = jnp.sum(weights * db_ref[...], axis=1, keepdims=True)


def attention_kernel(
    grad_ref, qkv_ref, h_ref, cos_ref, sin_ref, seg_row_ref, seg_col_ref, w_out_ref, w_ref,
    branch_ref, dmlp_ref, gain_ref,
    out_ref, dnorm_ref, dw_out_ref, dw_ref, db_ref, dot_ref, shift_ref,
    out_acc, acc,
):
    step = pl.program_id(0)
    grad = grad_ref[...]
    d_att = times_transpose(grad, w_out_ref[...]).astype(BF16)
    seg_rows, seg_cols = seg_col_ref[...], seg_row_ref[0]
    row_index = lax.broadcasted_iota(jnp.int32, (SLOTS, SLOTS), 0)
    col_index = lax.broadcasted_iota(jnp.int32, (SLOTS, SLOTS), 1)
    allowed = ((seg_rows == seg_cols) & (seg_cols >= 0) & (col_index <= row_index)) | (
        col_index == row_index
    )
    attended, d_query, d_key, d_value = [], [], [], []
    for head in range(2):
        query = qkv_ref[:, 64 * head : 64 * head + 64]
        key = qkv_ref[:, 128 + 64 * head : 192 + 64 * head]
        value = qkv_ref[:, 256 + 64 * head : 320 + 64 * head]
        d_head = d_att[:, 64 * head : 64 * head + 64]
        scores = jnp.where(allowed, times_transpose(query, key) * HEAD_DIM ** (-0.5), -1e30)
        weights = jnp.exp(scores - jnp.max(scores, axis=-1, keepdims=True))
        prob = weights * (1.0 / jnp.sum(weights, axis=-1, keepdims=True))
        prob_low = prob.astype(BF16)
        attended.append(plain(prob_low, value))
        d_prob = times_transpose(d_head, value)
        row_dot = jnp.sum(prob * d_prob, axis=-1, keepdims=True)
        d_score = (prob * (d_prob - row_dot)).astype(BF16)
        d_query.append(plain(d_score, key) * HEAD_DIM ** (-0.5))
        d_key.append(inner_rows(d_score, query) * HEAD_DIM ** (-0.5))
        d_value.append(inner_rows(prob_low, d_head))
    cos_rows, sin_rows = cos_ref[...], sin_ref[...]
    turned = []
    for parts in (d_query, d_key):
        rows = jnp.concatenate(parts, axis=1)
        turned.append(rows * cos_rows - swap_pairs(rows) * sin_rows)
    att_low = jnp.concatenate(attended, axis=1).astype(BF16)
    d_joined = jnp.concatenate(turned + d_value, axis=1).astype(BF16)
    out_ref[...] = (plain(att_low, w_out_ref[...]) + branch_ref[...].astype(F32)).astype(BF16)
    dnorm_ref[...] = (
        times_transpose(d_joined, w_ref[...]) * gain_ref[...] + dmlp_ref[...].astype(F32)
    ).astype(BF16)
    accumulate(db_ref, step, jnp.sum(d_joined.astype(F32), axis=0, keepdims=True))
    accumulate(out_acc, step, inner_rows(att_low, grad))
    accumulate(acc, step, inner_rows(h_ref[...], d_joined))

    @pl.when(step == pl.num_programs(0) - 1)
    def _():
        dw_out_ref[...] = out_acc[...].astype(BF16)
        dw_ref[...] = acc[...].astype(BF16)
        weights = w_ref[...].astype(F32)
        dot_ref[...] = jnp.sum(weights * acc[...], axis=1, keepdims=True)
        shift_ref[...] = jnp.sum(weights * db_ref[...], axis=1, keepdims=True)


def tiled(width):
    return pl.BlockSpec((SLOTS, width), lambda i: (i, 0))


def kept(shape):
    return pl.BlockSpec(shape, lambda i: (0,) * len(shape))


def shaped(shape, dtype):
    return jax.ShapeDtypeStruct(shape, dtype)


def run(kernel, operands, in_specs, outs, out_specs, scratch, flops, moved, name):
    return pl.pallas_call(
        kernel,
        grid=(PLANE,),
        in_specs=in_specs,
        out_specs=out_specs,
        out_shape=outs,
        scratch_shapes=scratch,
        compiler_params=pltpu.CompilerParams(
            vmem_limit_bytes=VMEM_BYTES, dimension_semantics=("arbitrary",)
        ),
        cost_estimate=pl.CostEstimate(flops=flops, bytes_accessed=moved, transcendentals=0),
        name=name,
    )(*operands)


def run_up(held, w_up, gain, shift, bias):
    return run(
        up_kernel,
        (held, w_up, gain, shift, bias),
        [tiled(D), kept((D, FF_PART)), kept((1, D)), kept((1, D)), kept((1, FF_PART))],
        [
            shaped((HELD, D), BF16),
            shaped((HELD, FF_PART), BF16),
            shaped((HELD, FF_PART), F32),
        ],
        [tiled(D), tiled(FF_PART), tiled(FF_PART)],
        [],
        2 * HELD * D * FF_PART,
        HELD * (4 * D + 6 * FF_PART),
        "up",
    )


def run_qkv(held, w_qkv, gain, shift, bias, cos_rows, sin_rows):
    return run(
        qkv_kernel,
        (held, w_qkv, gain, shift, bias, cos_rows, sin_rows),
        [
            tiled(D),
            kept((D, QKV_PART)),
            kept((1, D)),
            kept((1, D)),
            kept((1, QKV_PART)),
            tiled(128),
            tiled(128),
        ],
        [shaped((HELD, D), BF16), shaped((HELD, QKV_PART), BF16)],
        [tiled(D), tiled(QKV_PART)],
        [],
        2 * HELD * D * QKV_PART,
        HELD * (4 * D + 2 * QKV_PART + 1024),
        "qkv",
    )


def run_down(grad, h_mlp, hidden, slope, w_down, w_up, gain):
    return run(
        down_kernel,
        (grad, h_mlp, hidden, slope, w_down, w_up, gain),
        [
            tiled(D),
            tiled(D),
            tiled(FF_PART),
            tiled(FF_PART),
            kept((FF_PART, D)),
            kept((D, FF_PART)),
            kept((1, D)),
        ],
        [
            shaped((HELD, D), BF16),
            shaped((HELD, D), BF16),
            shaped((FF_PART, D), BF16),
            shaped((D, FF_PART), BF16),
            shaped((1, FF_PART), F32),
            shaped((D, 1), F32),
            shaped((D, 1), F32),
        ],
        [
            tiled(D),
            tiled(D),
            kept((FF_PART, D)),
            kept((D, FF_PART)),
            kept((1, FF_PART)),
            kept((D, 1)),
            kept((D, 1)),
        ],
        [pltpu.VMEM((FF_PART, D), F32), pltpu.VMEM((D, FF_PART), F32)],
        10 * HELD * D * FF_PART,
        HELD * (8 * D + 6 * FF_PART),
        "down",
    )


def run_attention(
    grad, qkv, h_attn, cos_rows, sin_rows, segments, w_out, w_qkv, branch, dmlp, gain
):
    return run(
        attention_kernel,
        (
            grad, qkv, h_attn, cos_rows, sin_rows,
            segments.reshape(PLANE, 1, SLOTS), segments.reshape(HELD, 1),
            w_out, w_qkv, branch, dmlp, gain,
        ),
        [
            tiled(D),
            tiled(QKV_PART),
            tiled(D),
            tiled(128),
            tiled(128),
            pl.BlockSpec((1, 1, SLOTS), lambda i: (i, 0, 0)),
            tiled(1),
            kept((128, D)),
            kept((D, QKV_PART)),
            tiled(D),
            tiled(D),
            kept((1, D)),
        ],
        [
            shaped((HELD, D), BF16),
            shaped((HELD, D), BF16),
            shaped((128, D), BF16),
            shaped((D, QKV_PART), BF16),
            shaped((1, QKV_PART), F32),
            shaped((D, 1), F32),
            shaped((D, 1), F32),
        ],
        [
            tiled(D),
            tiled(D),
            kept((128, D)),
            kept((D, QKV_PART)),
            kept((1, QKV_PART)),
            kept((D, 1)),
            kept((D, 1)),
        ],
        [pltpu.VMEM((128, D), F32), pltpu.VMEM((D, QKV_PART), F32)],
        4 * HELD * D * (QKV_PART + 128) + 24 * HELD * SLOTS * 256,
        HELD * 12 * D,
        "attention",
    )


def rotary_rows(segments):
    index = jnp.arange(SLOTS, dtype=jnp.int32)[None, :]
    start = jnp.zeros_like(segments)
    for number in range(-1, 4):
        first = jnp.min(jnp.where(segments == number, index, SLOTS), axis=1, keepdims=True)
        start = jnp.where(segments == number, first, start)
    position = (index - start).astype(F32).reshape(HELD, 1)
    lane = jnp.arange(128, dtype=jnp.int32) % HEAD_DIM
    inv_freq = 10000.0 ** (-(lane % 8).astype(F32) * 2.0 / ROTARY)
    angles = position * jnp.where(lane < ROTARY, inv_freq, 0.0)[None, :]
    sign = jnp.where(lane < ROTARY // 2, -1.0, 1.0)
    return (jnp.cos(angles), jnp.sin(angles) * sign[None, :])


def on_device_plane(
    tokens, segment_ids, cotangent, w_qkv, w_out, w_up, w_down,
    b_qkv, b_out, b_up, b_down, gain_attn, shift_attn, gain_mlp, shift_mlp,
):
    me = lax.axis_index("fsdp")
    rank, core, chip = me % PLANE, me % 2, (me % PLANE) // 2
    rows = w_up.shape[0]

    up_cuts = w_up.reshape(rows, LINE, PLANE, 128).transpose(2, 0, 1, 3)
    qkv_cuts = w_qkv.reshape(rows, 3, 2, 2, 4, HEAD_DIM).transpose(4, 2, 0, 1, 3, 5)
    vectors = jnp.concatenate(
        [b_qkv, b_out, b_up, b_down, gain_attn, shift_attn, gain_mlp, shift_mlp]
    )
    block = jnp.concatenate(
        [
            jnp.pad(vectors, (0, 512 - vectors.shape[0])).reshape(4, 128),
            segment_ids.astype(BF16).reshape(4, 128),
            jnp.zeros((rows - 8, 128), BF16),
        ]
    )
    got = over_plane(
        jnp.concatenate(
            [
                up_cuts.reshape(PLANE, rows, FF_PART),
                jnp.broadcast_to(block[None], (PLANE, rows, 128)),
                qkv_cuts.reshape(PLANE, rows, QKV_PART),
            ],
            axis=2,
        )
    ).reshape(PLANE * rows, 1024)
    up_all = gather_line(got[:, :640]).reshape(D, 640)
    down_all = gather_line(jnp.concatenate([w_down, w_out]))
    qkv_part = gather_line(got[:, 640:]).reshape(D, QKV_PART)
    up_part = up_all[:, :FF_PART]
    down_part = down_all[:, :128].reshape(FF_PART, D)

    held = spread_tokens(tokens)
    live_rows = (segment_ids >= 0).astype(F32)
    grad_out = cotangent.astype(F32) * live_rows[:, None]
    grad_own = grad_out.astype(BF16)
    grad = spread_tokens(grad_own)

    halves = down_all[:, 128:]
    mine = lax.dynamic_slice_in_dim(halves, 2 * core, 2)
    theirs = swap_core(lax.dynamic_slice_in_dim(halves, 2 - 2 * core, 2))
    out_part = jnp.where(
        core == 0, jnp.stack([mine, theirs], axis=1), jnp.stack([theirs, mine], axis=1)
    ).reshape(128, D)

    vec = up_all[:, FF_PART:].reshape(DEVICES, rows, 128)[:, :4].reshape(DEVICES, 512)
    vec = vec.astype(F32)
    qkv_bias = vec[:, :96].reshape(3, 2, 2, 4, HEAD_DIM)
    qkv_bias = lax.dynamic_index_in_dim(qkv_bias, chip, 3, keepdims=False)
    qkv_bias = lax.dynamic_index_in_dim(qkv_bias, core, 1, keepdims=False).reshape(1, QKV_PART)
    up_bias = vec[:, 128:256].reshape(LINE, PLANE, 128)
    up_bias = lax.dynamic_index_in_dim(up_bias, rank, 1, keepdims=False).reshape(1, FF_PART)
    out_bias = (vec[:, 96:128] + vec[:, 256:288]).reshape(1, D)
    gain_one, shift_one, gain_two, shift_two = (
        vec[:, 288 + 32 * i : 320 + 32 * i].reshape(1, D) for i in range(4)
    )

    near = 2 + 2 * core
    far = 6 - near
    order = jnp.stack(
        [
            rank, rank ^ near, rank ^ far, rank ^ 6,
            rank ^ 1, rank ^ 1 ^ far, rank ^ 1 ^ near, rank ^ 7,
        ]
    )
    seg_all = got[:, FF_PART:640].reshape(PLANE, rows, 128)[:, 4:8].reshape(PLANE, SLOTS)
    segments = jnp.take(seg_all, order, axis=0).astype(jnp.int32)
    cos_rows, sin_rows = rotary_rows(segments)

    h_mlp, hidden, slope = run_up(held, up_part, gain_two, shift_two, up_bias)
    h_attn, qkv = run_qkv(held, qkv_part, gain_one, shift_one, qkv_bias, cos_rows, sin_rows)
    branch, dmlp, dw_down, dw_up, db_up, dot_two, sum_two = run_down(
        grad, h_mlp, hidden, slope, down_part, up_part, gain_two
    )
    out_sum, dnorm_sum, dw_out, dw_qkv, db_qkv, dot_one, sum_one = run_attention(
        grad, qkv, h_attn, cos_rows, sin_rows, segments, out_part, qkv_part, branch, dmlp, gain_one
    )

    grad_w_down = sum_line(dw_down.reshape(LINE, 128, D))
    up_rows = sum_line(dw_up.reshape(LINE, PLANE * rows, FF_PART)).astype(BF16)
    up_rows = over_plane(up_rows.reshape(PLANE, rows, FF_PART))
    grad_w_up = (
        up_rows.reshape(PLANE, rows, LINE, 128).transpose(1, 2, 0, 3).reshape(rows, 4 * D)
    ).astype(F32)

    pieces = dw_out.reshape(2, 2, 32, D)
    mine = lax.dynamic_index_in_dim(pieces, core, 1, keepdims=False)
    theirs = swap_core(lax.dynamic_index_in_dim(pieces, 1 - core, 1, keepdims=False))
    pieces = jnp.where(
        core == 0, jnp.concatenate([mine, theirs]), jnp.concatenate([theirs, mine])
    )
    pieces = pieces.reshape(LINE, 32, 8, 128).transpose(0, 2, 1, 3).reshape(LINE, 256, 128)
    last = sum_line(
        jnp.concatenate([dw_qkv.reshape(LINE, PLANE * rows, QKV_PART), pieces], axis=2)
    )
    grad_w_out = last[:, QKV_PART:].reshape(8, 32, 128).transpose(1, 0, 2).reshape(32, D)
    qkv_rows = over_plane(last[:, :QKV_PART].astype(BF16).reshape(PLANE, rows, QKV_PART))
    grad_w_qkv = (
        qkv_rows.reshape(4, 2, rows, 3, 2, HEAD_DIM)
        .transpose(2, 3, 1, 4, 0, 5)
        .reshape(rows, 3 * D)
        .astype(F32)
    )

    def at(index, count):
        return (jnp.arange(count) == index).astype(F32)

    db_qkv = db_qkv.reshape(3, 1, 2, 1, HEAD_DIM)
    db_qkv = db_qkv * at(core, 2)[:, None, None, None] * at(chip, 4)[:, None]
    db_up = db_up.reshape(LINE, 1, 128) * at(rank, PLANE)[:, None]
    dot_one, sum_one = dot_one.reshape(1, D), sum_one.reshape(1, D)
    dot_two, sum_two = dot_two.reshape(1, D), sum_two.reshape(1, D)
    sums = jnp.concatenate(
        [
            db_qkv.reshape(DEVICES, 96),
            column_sums(grad_own).reshape(DEVICES, 32),
            db_up.reshape(DEVICES, 128),
            ((dot_one - shift_one * sum_one) / gain_one).reshape(DEVICES, 32),
            sum_one.reshape(DEVICES, 32),
            ((dot_two - shift_two * sum_two) / gain_two).reshape(DEVICES, 32),
            sum_two.reshape(DEVICES, 32),
        ],
        axis=1,
    )
    sums = over_groups(sums.reshape(DEVICES, 3, 128), None)
    sums = jnp.sum(sums, axis=0).reshape(384)

    inputs = tokens.astype(F32)
    layer_out = (inputs + collect_tokens(out_sum) + out_bias).astype(BF16)
    normed, inv_scale = normalize(inputs)
    d_norm = collect_tokens(dnorm_sum)
    d_inner = (
        d_norm
        - jnp.mean(d_norm, axis=-1, keepdims=True)
        - normed * jnp.mean(d_norm * normed, axis=-1, keepdims=True)
    )
    tokens_grad = grad_out + d_inner * inv_scale
    return (
        layer_out,
        tokens_grad,
        grad_w_qkv,
        grad_w_out,
        grad_w_up,
        grad_w_down,
        sums[:96],
        sums[96:128],
        sums[128:256],
        sums[96:128],
        sums[256:288],
        sums[288:320],
        sums[320:352],
        sums[352:384],
    )


def choose(mesh):
    return on_device_plane if mesh.shape["fsdp"] == DEVICES else on_device_any


def solution(mesh):
    in_specs = (
        P("fsdp", None),
        P("fsdp"),
        P("fsdp", None),
        P("fsdp", None),
        P("fsdp", None),
        P("fsdp", None),
        P("fsdp", None),
        P("fsdp"),
        P("fsdp"),
        P("fsdp"),
        P("fsdp"),
        P("fsdp"),
        P("fsdp"),
        P("fsdp"),
        P("fsdp"),
    )
    out_specs = (
        P("fsdp", None),
        P("fsdp", None),
        P("fsdp", None),
        P("fsdp", None),
        P("fsdp", None),
        P("fsdp", None),
        P("fsdp"),
        P("fsdp"),
        P("fsdp"),
        P("fsdp"),
        P("fsdp"),
        P("fsdp"),
        P("fsdp"),
        P("fsdp"),
    )
    return jax.shard_map(
        choose(mesh), mesh=mesh, in_specs=in_specs, out_specs=out_specs, check_vma=False
    )
```

```python
from functools import partial

import jax
import jax.numpy as jnp
from jax import lax
from jax.experimental import pallas as pl
from jax.experimental.pallas import tpu as pltpu
from jax.sharding import PartitionSpec as P

D = 1024
HEADS = 16
HEAD_DIM = 64
ROTARY = 16


epsilon = 1e-05


def rotary_tables(position):
    inv_freq = 10000.0 ** (-jnp.arange(ROTARY // 2, dtype=jnp.float32) * 2.0 / ROTARY)
    angles = position[:, None] * inv_freq[None, :]
    return (jnp.cos(angles)[:, None, :], jnp.sin(angles)[:, None, :])


def rotate(features, cos_table, sin_table):
    half_dims = ROTARY // 2
    lower_half = features[..., :half_dims]
    upper_half = features[..., half_dims:ROTARY]
    return jnp.concatenate(
        [
            lower_half * cos_table - upper_half * sin_table,
            upper_half * cos_table + lower_half * sin_table,
            features[..., ROTARY:],
        ],
        axis=-1,
    )


def allowed_mask(seg_rows, seg_cols, row_index, col_index):
    same_seq = (
        (seg_rows[:, None] == seg_cols[None, :])
        & (seg_cols[None, :] >= 0)
        & (col_index[None, :] <= row_index[:, None])
    )
    return same_seq | (col_index[None, :] == row_index[:, None])


def inner_rows(left_side, right_side):
    return lax.dot_general(
        left_side, right_side, (((0,), (0,)), ((), ())), preferred_element_type=jnp.float32
    )


def times_transpose(left_side, right_side):
    return lax.dot_general(
        left_side, right_side, (((1,), (1,)), ((), ())), preferred_element_type=jnp.float32
    )


def block_scores(query_block, key_part, segment_ids, tok_index):
    raw_scores = jnp.einsum(
        "qhd,khd->hqk", query_block, key_part, preferred_element_type=jnp.float32
    ) * HEAD_DIM ** (-0.5)
    allowed = allowed_mask(segment_ids, segment_ids, tok_index, tok_index)
    return jnp.where(allowed[None], raw_scores, -1e30)


def column_sums(values):
    return jnp.sum(values.astype(jnp.float32), axis=0)


def on_device_any(
    tokens,
    segment_ids,
    cotangent,
    w_qkv,
    w_out,
    w_up,
    w_down,
    b_qkv,
    b_out,
    b_up,
    b_down,
    gain_attn,
    shift_attn,
    gain_mlp,
    shift_mlp,
):
    gathered = (
        lax.all_gather(w_qkv, "fsdp", axis=0, tiled=True),
        lax.all_gather(w_out, "fsdp", axis=0, tiled=True),
        lax.all_gather(w_up, "fsdp", axis=0, tiled=True),
        lax.all_gather(w_down, "fsdp", axis=0, tiled=True),
        lax.all_gather(b_qkv, "fsdp", axis=0, tiled=True),
        lax.all_gather(b_out, "fsdp", axis=0, tiled=True),
        lax.all_gather(b_up, "fsdp", axis=0, tiled=True),
        lax.all_gather(b_down, "fsdp", axis=0, tiled=True),
        lax.all_gather(gain_attn, "fsdp", axis=0, tiled=True),
        lax.all_gather(shift_attn, "fsdp", axis=0, tiled=True),
        lax.all_gather(gain_mlp, "fsdp", axis=0, tiled=True),
        lax.all_gather(shift_mlp, "fsdp", axis=0, tiled=True),
    )
    wqkv_all, wout_all, wup_all, wdown_all = (gathered[0], gathered[1], gathered[2], gathered[3])
    bias_qkv = gathered[4].astype(jnp.float32)
    bias_out = gathered[5].astype(jnp.float32)
    bias_up = gathered[6].astype(jnp.float32)
    bias_down = gathered[7].astype(jnp.float32)
    gain_one = gathered[8].astype(jnp.float32)
    shift_one = gathered[9].astype(jnp.float32)
    gain_two = gathered[10].astype(jnp.float32)
    shift_two = gathered[11].astype(jnp.float32)
    tok_count = tokens.shape[0]
    tok_index = jnp.arange(tok_count, dtype=jnp.int32)
    same_seq = segment_ids[:, None] == segment_ids[None, :]
    seq_start = jnp.min(jnp.where(same_seq, tok_index[None, :], tok_count), axis=1)
    position = (tok_index - seq_start).astype(jnp.float32)
    cos_table, sin_table = rotary_tables(position)
    inputs = tokens.astype(jnp.float32)
    center = inputs - jnp.mean(inputs, axis=-1, keepdims=True)
    inv_scale = lax.rsqrt(jnp.mean(center * center, axis=-1, keepdims=True) + epsilon)
    normed = center * inv_scale
    h_attn = (normed * gain_one + shift_one).astype(jnp.bfloat16)
    h_mlp = (normed * gain_two + shift_two).astype(jnp.bfloat16)
    joined = jnp.dot(h_attn, wqkv_all, preferred_element_type=jnp.float32) + bias_qkv
    query_rot = rotate(
        joined[:, :D].reshape(tok_count, HEADS, HEAD_DIM), cos_table, sin_table
    ).astype(jnp.bfloat16)
    key_rot = rotate(
        joined[:, D : 2 * D].reshape(tok_count, HEADS, HEAD_DIM), cos_table, sin_table
    ).astype(jnp.bfloat16)
    value_low = joined[:, 2 * D :].reshape(tok_count, HEADS, HEAD_DIM).astype(jnp.bfloat16)
    block_rows = min(512, tok_count)
    scores = block_scores(query_rot, key_rot, segment_ids, tok_index)
    row_max = jnp.max(scores, axis=-1, keepdims=True)
    weights = jnp.exp(scores - row_max)
    row_sum = jnp.sum(weights, axis=-1, keepdims=True)
    attn_prob = (weights / row_sum).astype(jnp.bfloat16)
    attended_blocks = jnp.einsum(
        "hqk,khd->qhd", attn_prob, value_low, preferred_element_type=jnp.float32
    )
    attended = attended_blocks.reshape(tok_count, D).astype(jnp.bfloat16)
    branch_attn = jnp.dot(attended, wout_all, preferred_element_type=jnp.float32) + bias_out
    pre_up = jnp.dot(h_mlp, wup_all, preferred_element_type=jnp.float32) + bias_up
    gelu_value, gelu_pull = jax.vjp(partial(jax.nn.gelu, approximate=False), pre_up)
    hidden = gelu_value.astype(jnp.bfloat16)
    branch_mlp = jnp.dot(hidden, wdown_all, preferred_element_type=jnp.float32) + bias_down
    layer_out = (inputs + branch_attn + branch_mlp).astype(jnp.bfloat16)
    again = (
        lax.all_gather(w_qkv, "fsdp", axis=0, tiled=True),
        lax.all_gather(w_out, "fsdp", axis=0, tiled=True),
        lax.all_gather(w_up, "fsdp", axis=0, tiled=True),
        lax.all_gather(w_down, "fsdp", axis=0, tiled=True),
        lax.all_gather(gain_attn, "fsdp", axis=0, tiled=True),
        lax.all_gather(gain_mlp, "fsdp", axis=0, tiled=True),
    )
    wqkv_bwd, wout_bwd, wup_bwd, wdown_bwd = (again[0], again[1], again[2], again[3])
    gain_one_bwd = again[4].astype(jnp.float32)
    gain_two_bwd = again[5].astype(jnp.float32)
    live_rows = (segment_ids >= 0).astype(jnp.float32)
    grad_out = cotangent.astype(jnp.float32) * live_rows[:, None]
    grad_low = grad_out.astype(jnp.bfloat16)
    grad_bias_out = column_sums(grad_low)
    grad_wout = inner_rows(attended, grad_low)
    grad_wdown = inner_rows(hidden, grad_low)
    d_hidden = times_transpose(grad_low, wdown_bwd)
    d_pre = gelu_pull(d_hidden)[0].astype(jnp.bfloat16)
    grad_bias_up = column_sums(d_pre)
    grad_wup = inner_rows(h_mlp, d_pre)
    d_h_mlp = times_transpose(d_pre, wup_bwd)
    grad_gain_mlp = jnp.sum(d_h_mlp * normed, axis=0)
    grad_shift_mlp = jnp.sum(d_h_mlp, axis=0)
    d_att = (
        times_transpose(grad_low, wout_bwd).astype(jnp.bfloat16).reshape(tok_count, HEADS, HEAD_DIM)
    )
    key_grad = jnp.zeros((tok_count, HEADS, HEAD_DIM), jnp.float32)
    value_grad = jnp.zeros((tok_count, HEADS, HEAD_DIM), jnp.float32)
    scores = block_scores(query_rot, key_rot, segment_ids, tok_index)
    attn_prob = jnp.exp(scores - row_max) / row_sum
    d_prob = jnp.einsum("qhd,khd->hqk", d_att, value_low, preferred_element_type=jnp.float32)
    row_dot = jnp.sum(attn_prob * d_prob, axis=-1, keepdims=True)
    d_score = (attn_prob * (d_prob - row_dot)).astype(jnp.bfloat16)
    query_grads = jnp.einsum(
        "hqk,khd->qhd", d_score, key_rot, preferred_element_type=jnp.float32
    ) * HEAD_DIM ** (-0.5)
    key_grad = key_grad.at[:block_rows].add(
        jnp.einsum("hqk,qhd->khd", d_score, query_rot, preferred_element_type=jnp.float32)
        * HEAD_DIM ** (-0.5)
    )
    value_grad = value_grad.at[:block_rows].add(
        jnp.einsum(
            "hqk,qhd->khd",
            attn_prob.astype(jnp.bfloat16),
            d_att,
            preferred_element_type=jnp.float32,
        )
    )
    query_grad = rotate(query_grads, cos_table, -sin_table)
    key_grad = rotate(key_grad, cos_table, -sin_table)
    d_joined = jnp.concatenate(
        [
            query_grad.reshape(tok_count, D),
            key_grad.reshape(tok_count, D),
            value_grad.reshape(tok_count, D),
        ],
        axis=1,
    ).astype(jnp.bfloat16)
    grad_bias_qkv = column_sums(d_joined)
    grad_wqkv = inner_rows(h_attn, d_joined)
    d_h_attn = times_transpose(d_joined, wqkv_bwd)
    grad_gain_attn = jnp.sum(d_h_attn * normed, axis=0)
    grad_shift_attn = jnp.sum(d_h_attn, axis=0)
    d_norm = d_h_attn * gain_one_bwd + d_h_mlp * gain_two_bwd
    d_inner = (
        d_norm
        - jnp.mean(d_norm, axis=-1, keepdims=True)
        - normed * jnp.mean(d_norm * normed, axis=-1, keepdims=True)
    )
    tokens_grad = grad_out + d_inner * inv_scale
    all_sums = (
        lax.psum_scatter(grad_wqkv, "fsdp", scatter_dimension=0, tiled=True),
        lax.psum_scatter(grad_wout, "fsdp", scatter_dimension=0, tiled=True),
        lax.psum_scatter(grad_wup, "fsdp", scatter_dimension=0, tiled=True),
        lax.psum_scatter(grad_wdown, "fsdp", scatter_dimension=0, tiled=True),
        lax.psum_scatter(grad_bias_qkv, "fsdp", scatter_dimension=0, tiled=True),
        lax.psum_scatter(grad_bias_out, "fsdp", scatter_dimension=0, tiled=True),
        lax.psum_scatter(grad_bias_up, "fsdp", scatter_dimension=0, tiled=True),
        lax.psum_scatter(grad_gain_attn, "fsdp", scatter_dimension=0, tiled=True),
        lax.psum_scatter(grad_shift_attn, "fsdp", scatter_dimension=0, tiled=True),
        lax.psum_scatter(grad_gain_mlp, "fsdp", scatter_dimension=0, tiled=True),
        lax.psum_scatter(grad_shift_mlp, "fsdp", scatter_dimension=0, tiled=True),
    )
    return (
        layer_out,
        tokens_grad,
        all_sums[0],
        all_sums[1],
        all_sums[2],
        all_sums[3],
        all_sums[4],
        all_sums[5],
        all_sums[6],
        all_sums[5],
        all_sums[7],
        all_sums[8],
        all_sums[9],
        all_sums[10],
    )


BF16 = jnp.bfloat16
F32 = jnp.float32
PLANE = 8
LINE = 4
DEVICES = PLANE * LINE
SLOTS = 512
HELD = PLANE * SLOTS
FF_PART = 512
QKV_PART = 384
VMEM_BYTES = 56 * 1024 * 1024


def exchange(values, partner):
    return lax.ppermute(values, "fsdp", [(i, partner(i)) for i in range(DEVICES)])


def swap_core(values):
    return exchange(values, lambda i: i ^ 1)


def swap_near(values):
    return exchange(values, lambda i: i ^ (4 if i % 2 else 2))


def swap_far(values):
    return exchange(values, lambda i: i ^ (2 if i % 2 else 4))


def over_groups(values, groups):
    return lax.all_to_all(
        values, "fsdp", split_axis=0, concat_axis=0, tiled=True, axis_index_groups=groups
    )


def over_plane(values):
    return over_groups(values, [[PLANE * z + r for r in range(PLANE)] for z in range(LINE)])


def line_near(values):
    return exchange(values, lambda i: i ^ (16 if i % 2 else 8))


def line_far(values):
    return exchange(values, lambda i: i ^ (8 if i % 2 else 16))


def gather_line(values):
    pair = jnp.stack([values, line_near(values)])
    return (pair, line_far(pair))


def finish(half):
    return half[0].astype(F32) + line_near(half[1]).astype(F32)


def add_low(left_side, right_side):
    return (left_side.astype(F32) + right_side.astype(F32)).astype(BF16)


def together(*values):
    return lax.optimization_barrier(values)


def normalize(rows):
    center = rows - jnp.mean(rows, axis=-1, keepdims=True)
    inv_scale = lax.rsqrt(jnp.mean(center * center, axis=-1, keepdims=True) + epsilon)
    return (center * inv_scale, inv_scale)


def plain(left_side, right_side):
    return lax.dot_general(
        left_side, right_side, (((1,), (0,)), ((), ())), preferred_element_type=F32
    )


def swap_pairs(values):
    lane = lax.broadcasted_iota(jnp.int32, values.shape, 1)
    return jnp.where(
        (lane & 8) == 0, pltpu.roll(values, 120, axis=1), pltpu.roll(values, 8, axis=1)
    )


def cut_kernel(up_ref, qkv_ref, out_ref):
    for rank in range(PLANE):
        for z in range(LINE):
            out_ref[rank, :, 128 * z : 128 * z + 128] = up_ref[
                :, 128 * (PLANE * z + rank) : 128 * (PLANE * z + rank) + 128
            ]
        for part in range(3):
            heads = [8 * (rank % 2) + 4 * i + rank // 2 for i in range(2)]
            out_ref[rank, :, FF_PART + 128 * part : FF_PART + 128 * part + 128] = jnp.concatenate(
                [qkv_ref[:, D * part + 64 * h : D * part + 64 * h + 64] for h in heads], axis=1
            )


def place_up_kernel(rows_ref, out_ref):
    for rank in range(PLANE):
        for z in range(LINE):
            out_ref[:, 128 * (PLANE * z + rank) : 128 * (PLANE * z + rank) + 128] = rows_ref[
                rank, :, 128 * z : 128 * z + 128
            ].astype(F32)


def place_qkv_kernel(rows_ref, out_ref):
    def cut(part, head):
        rank, slot = 2 * (head % 4) + head // 8, head // 4 % 2
        start = 128 * part + 64 * slot
        return rows_ref[rank, :, start : start + 64].astype(F32)

    for part in range(3):
        for head in range(0, HEADS, 2):
            start = D * part + 64 * head
            out_ref[:, start : start + 128] = jnp.concatenate(
                [cut(part, head), cut(part, head + 1)], axis=1
            )


def whole(kernel, out, *operands):
    return pl.pallas_call(
        kernel,
        out_shape=out,
        compiler_params=pltpu.CompilerParams(vmem_limit_bytes=VMEM_BYTES),
    )(*operands)


def assemble(place_ref, pair_ref, far_ref, out_ref):
    count = pair_ref.shape[1]
    for z in range(LINE):
        place = place_ref[z]
        rows = slice(count * z, count * z + count)

        @pl.when(place < 2)
        def _():
            out_ref[rows, :] = pair_ref[jnp.minimum(place, 1)]

        @pl.when(place >= 2)
        def _():
            out_ref[rows, :] = far_ref[jnp.maximum(place - 2, 0)]


def cut_line(order_ref, total_ref, out_ref):
    count = out_ref.shape[1]
    for piece in range(LINE):
        start = pl.multiple_of(order_ref[piece] * count, count)
        out_ref[piece] = total_ref[pl.ds(start, count), :].astype(BF16)


def pick(step, half_ref, other_ref):
    return jnp.where(step < 2, half_ref[...], other_ref[...])


def put(step, half_ref, other_ref, value):
    @pl.when(step < 2)
    def _():
        half_ref[...] = value

    @pl.when(step >= 2)
    def _():
        other_ref[...] = value


def front_kernel(
    place_ref, tok_half, tok_other, pair_ref, far_ref, cos_ref, sin_ref, vec_ref, up_bias_ref,
    qkv_bias_ref, h_attn_ref, h_mlp_ref, hidden_ref, slope_ref, qkv_ref, w_ref,
):
    step = pl.program_id(0)

    @pl.when(step == 0)
    def _():
        assemble(place_ref, pair_ref, far_ref, w_ref)

    front_tile(
        pick(step, tok_half, tok_other), w_ref, cos_ref, sin_ref, vec_ref, up_bias_ref,
        qkv_bias_ref, h_attn_ref, h_mlp_ref, hidden_ref, slope_ref, qkv_ref,
    )


def front_again_kernel(
    tok_half, tok_other, w_ref, cos_ref, sin_ref, vec_ref, up_bias_ref, qkv_bias_ref,
    h_attn_ref, h_mlp_ref, hidden_ref, slope_ref, qkv_ref,
):
    front_tile(
        pick(pl.program_id(0), tok_half, tok_other), w_ref, cos_ref, sin_ref, vec_ref,
        up_bias_ref, qkv_bias_ref, h_attn_ref, h_mlp_ref, hidden_ref, slope_ref, qkv_ref,
    )


def front_tile(
    tok, w_ref, cos_ref, sin_ref, vec_ref, up_bias_ref, qkv_bias_ref,
    h_attn_ref, h_mlp_ref, hidden_ref, slope_ref, qkv_ref,
):
    normed, _ = normalize(tok.astype(F32))
    h_attn = (normed * vec_ref[0:1] + vec_ref[1:2]).astype(BF16)
    h_mlp = (normed * vec_ref[2:3] + vec_ref[3:4]).astype(BF16)
    h_attn_ref[...] = h_attn
    h_mlp_ref[...] = h_mlp
    pre = plain(h_mlp, w_ref[:, :FF_PART]) + up_bias_ref[...]
    cdf = 0.5 + 0.5 * lax.erf(pre * 0.5**0.5)
    hidden_ref[...] = (pre * cdf).astype(BF16)
    slope_ref[...] = (cdf + pre * jnp.exp(-0.5 * pre * pre) * 0.3989422804014327).astype(BF16)
    joined = plain(h_attn, w_ref[:, FF_PART:]) + qkv_bias_ref[...]
    cos_rows, sin_rows = cos_ref[...], sin_ref[...]
    for part in range(2):
        rows = joined[:, 128 * part : 128 * part + 128]
        rows = rows * cos_rows + swap_pairs(rows) * sin_rows
        if part == 0:
            rows = rows * HEAD_DIM ** (-0.5)
        qkv_ref[:, 128 * part : 128 * part + 128] = rows.astype(BF16)
    qkv_ref[:, 256:] = joined[:, 256:].astype(BF16)


def accumulate(total_ref, step, value, prev_ref=None):
    @pl.when(step == 0)
    def _():
        total_ref[...] = value if prev_ref is None else value + prev_ref[...]

    @pl.when(step > 0)
    def _():
        total_ref[...] += value


def mlp_tile(step, grad, h, hidden, slope, w_down, w_up, d_pre_ref, totals, prev):
    d_low = (times_transpose(grad, w_down) * slope.astype(F32)).astype(BF16)
    d_pre_ref[...] = d_low
    accumulate(totals[0], step, inner_rows(d_low, h), prev[0])
    accumulate(totals[1], step, inner_rows(hidden, grad), prev[1])
    accumulate(totals[2], step, jnp.sum(d_low.astype(F32), axis=0, keepdims=True), prev[2])


def mlp_kernel(
    place_ref, grad_half, grad_other, h_ref, hidden_ref, slope_ref, pair_ref, far_ref, w_ref,
    d_pre_ref, w_down_ref, up_ref, down_ref, db_ref,
):
    step = pl.program_id(0)

    @pl.when(step == 0)
    def _():
        assemble(place_ref, pair_ref, far_ref, w_down_ref)

    mlp_tile(
        step, pick(step, grad_half, grad_other), h_ref[...], hidden_ref[...], slope_ref[...],
        w_down_ref[...], w_ref[:, :FF_PART], d_pre_ref, (up_ref, down_ref, db_ref), (None,) * 3,
    )


def mlp_last_kernel(
    order_ref, grad_half, grad_other, h_ref, hidden_ref, slope_ref, w_down_ref, w_ref,
    up_prev, down_prev, db_prev, d_pre_ref, dw_up_ref, dw_down_ref, db_ref, dot_ref, shift_ref,
    up_acc, down_acc,
):
    step = pl.program_id(0)
    w_up = w_ref[:, :FF_PART]
    mlp_tile(
        step, pick(step, grad_half, grad_other), h_ref[...], hidden_ref[...], slope_ref[...],
        w_down_ref[...], w_up, d_pre_ref, (up_acc, down_acc, db_ref),
        (up_prev, down_prev, db_prev),
    )

    @pl.when(step == pl.num_programs(0) - 1)
    def _():
        cut_line(order_ref, down_acc, dw_down_ref)
        total = up_acc[...].T
        up_acc_rows = total.astype(BF16)
        for piece in range(LINE):
            for z in range(LINE):
                @pl.when(order_ref[piece] == z)
                def _():
                    dw_up_ref[piece] = up_acc_rows[256 * z : 256 * z + 256]
        weights = w_up.astype(F32)
        dot_ref[...] = jnp.sum(weights * total, axis=1, keepdims=True)
        shift_ref[...] = jnp.sum(weights * db_ref[...], axis=1, keepdims=True)


def attend(qkv_ref, d_att, seg_rows, seg_cols):
    size = SLOTS // 2
    masks = []
    for block in range(2):
        count = size * (block + 1)
        row_index = lax.broadcasted_iota(jnp.int32, (size, count), 0) + size * block
        col_index = lax.broadcasted_iota(jnp.int32, (size, count), 1)
        rows = seg_rows[size * block : count]
        cols = seg_cols[:, :count]
        masks.append(
            ((rows == cols) & (cols >= 0) & (col_index <= row_index)) | (col_index == row_index)
        )
    attended, d_query, d_key, d_value = [], [], [], []
    for head in range(2):
        query = qkv_ref[:, 64 * head : 64 * head + 64]
        key = qkv_ref[:, 128 + 64 * head : 192 + 64 * head]
        value = qkv_ref[:, 256 + 64 * head : 320 + 64 * head]
        d_head = d_att[:, 64 * head : 64 * head + 64]
        att, dq, dk, dv = [], [], [], []
        for block in range(2):
            count = size * (block + 1)
            rows = slice(size * block, count)
            keys, values = key[:count], value[:count]
            scores = jnp.where(masks[block], times_transpose(query[rows], keys), -1e30)
            weights = jnp.exp(scores - jnp.max(scores, axis=-1, keepdims=True))
            prob = weights * (1.0 / jnp.sum(weights, axis=-1, keepdims=True))
            prob_low = prob.astype(BF16)
            att.append(plain(prob_low, values))
            d_prob = times_transpose(d_head[rows], values)
            row_dot = jnp.sum(prob * d_prob, axis=-1, keepdims=True)
            d_score = (prob * (d_prob - row_dot)).astype(BF16)
            dq.append(plain(d_score, keys) * HEAD_DIM ** (-0.5))
            dk.append(inner_rows(d_score, query[rows]))
            dv.append(inner_rows(prob_low, d_head[rows]))
        attended.append(jnp.concatenate(att))
        d_query.append(jnp.concatenate(dq))
        d_key.append(jnp.concatenate([dk[1][:size] + dk[0], dk[1][size:]]))
        d_value.append(jnp.concatenate([dv[1][:size] + dv[0], dv[1][size:]]))
    return [jnp.concatenate(parts, axis=1) for parts in (attended, d_query, d_key, d_value)]


def attention_kernel(
    grad_half, grad_other, qkv_ref, h_ref, hidden_ref, d_pre_ref, cos_ref, sin_ref,
    seg_row_ref, seg_col_ref, w_out_ref, w_ref, w_down_ref, vec_ref, prev,
    out_half, out_other, norm_half, norm_other, out_acc, acc, db_ref,
):
    step = pl.program_id(0)
    grad = pick(step, grad_half, grad_other)
    d_att = times_transpose(grad, w_out_ref[...]).astype(BF16)
    attended, d_query, d_key, d_value = attend(qkv_ref, d_att, seg_col_ref[...], seg_row_ref[0])
    cos_rows, sin_rows = cos_ref[...], sin_ref[...]
    d_query = d_query * cos_rows - swap_pairs(d_query) * sin_rows
    d_key = d_key * cos_rows - swap_pairs(d_key) * sin_rows
    att_low = attended.astype(BF16)
    d_joined = jnp.concatenate([d_query, d_key, d_value], axis=1).astype(BF16)
    put(
        step,
        out_half,
        out_other,
        (plain(att_low, w_out_ref[...]) + plain(hidden_ref[...], w_down_ref[...])).astype(BF16),
    )
    put(
        step,
        norm_half,
        norm_other,
        (
            times_transpose(d_joined, w_ref[:, FF_PART:]) * vec_ref[0:1]
            + times_transpose(d_pre_ref[...], w_ref[:, :FF_PART]) * vec_ref[2:3]
        ).astype(BF16),
    )
    accumulate(out_acc, step, inner_rows(att_low, grad), prev[0])
    accumulate(acc, step, inner_rows(h_ref[...], d_joined), prev[1])
    accumulate(db_ref, step, jnp.sum(d_joined.astype(F32), axis=0, keepdims=True), prev[2])


def attention_first_kernel(*refs):
    attention_kernel(*refs[:14], (None,) * 3, *refs[14:])


def attention_last_kernel(*refs):
    order_ref, ins, prev = refs[0], refs[1:15], refs[15:18]
    outs, (dw_out_ref, dw_ref, db_ref, dot_ref, shift_ref, out_acc, acc) = refs[18:22], refs[22:]
    attention_kernel(*ins, prev, *outs, out_acc, acc, db_ref)
    w_ref = ins[11]

    @pl.when(pl.program_id(0) == pl.num_programs(0) - 1)
    def _():
        dw_out_ref[...] = out_acc[...].astype(BF16)
        cut_line(order_ref, acc, dw_ref)
        weights = w_ref[:, FF_PART:].astype(F32)
        dot_ref[...] = jnp.sum(weights * acc[...], axis=1, keepdims=True)
        shift_ref[...] = jnp.sum(weights * db_ref[...], axis=1, keepdims=True)


STEPS = 4
GROUP = STEPS * SLOTS
COLUMNS = FF_PART + QKV_PART
SCALARS = pl.BlockSpec(memory_space=pltpu.SMEM)


def tiled(width):
    return pl.BlockSpec((SLOTS, width), lambda i: (i, 0))


def half_of(index):
    return pl.BlockSpec((SLOTS, D), lambda i: (jnp.clip(i - 2 * index, 0, 1), 0))


HALVES = [half_of(0), half_of(1)]


def kept(*shape):
    return pl.BlockSpec(shape, lambda i: (0,) * len(shape))


def whole_out(dtype, *shape):
    return (kept(*shape), shape, dtype)


def tiled_out(width):
    return (tiled(width), (GROUP, width), BF16)


def halves_out():
    return [(spec, (GROUP // 2, D), BF16) for spec in HALVES]


def run(kernel, name, operands, in_specs, outs, scratch, flops, moved):
    return pl.pallas_call(
        kernel,
        grid=(STEPS,),
        in_specs=in_specs,
        out_specs=[spec for spec, _, _ in outs],
        out_shape=[jax.ShapeDtypeStruct(shape, dtype) for _, shape, dtype in outs],
        scratch_shapes=[pltpu.VMEM(shape, F32) for shape in scratch],
        compiler_params=pltpu.CompilerParams(
            vmem_limit_bytes=VMEM_BYTES, dimension_semantics=("arbitrary",)
        ),
        cost_estimate=pl.CostEstimate(
            flops=2 * GROUP * D * flops, bytes_accessed=2 * GROUP * D * moved, transcendentals=0
        ),
        name=name,
    )(*operands)


def run_front(place, held, pieces, weights, cos_rows, sin_rows, vec, up_bias, qkv_bias):
    operands = (cos_rows, sin_rows, vec, up_bias, qkv_bias)
    specs = [tiled(128), tiled(128), kept(4, D), kept(1, FF_PART), kept(1, QKV_PART)]
    outs = [tiled_out(width) for width in (D, D, FF_PART, FF_PART, QKV_PART)]
    if weights is None:
        piece = kept(2, D // LINE, COLUMNS)
        return run(
            front_kernel, "front", (place, *held, *pieces, *operands),
            [SCALARS, *HALVES, piece, piece, *specs],
            [*outs, whole_out(BF16, D, COLUMNS)], [], COLUMNS, 5,
        )
    return run(
        front_again_kernel, "front", (*held, weights, *operands),
        [*HALVES, kept(D, COLUMNS), *specs], outs, [], COLUMNS, 5,
    )


def run_mlp(place, grad, h_mlp, hidden, slope, pieces, weights):
    piece = kept(2, FF_PART // LINE, D)
    return run(
        mlp_kernel, "mlp", (place, *grad, h_mlp, hidden, slope, *pieces, weights),
        [
            SCALARS, *HALVES, tiled(D), tiled(FF_PART), tiled(FF_PART), piece, piece,
            kept(D, COLUMNS),
        ],
        [
            tiled_out(FF_PART), whole_out(BF16, FF_PART, D), whole_out(F32, FF_PART, D),
            whole_out(F32, FF_PART, D), whole_out(F32, 1, FF_PART),
        ],
        [], 3 * FF_PART, 4,
    )


def run_mlp_last(order, grad, h_mlp, hidden, slope, w_down, weights, totals):
    return run(
        mlp_last_kernel, "mlp", (order, *grad, h_mlp, hidden, slope, w_down, weights, *totals),
        [
            SCALARS, *HALVES, tiled(D), tiled(FF_PART), tiled(FF_PART), kept(FF_PART, D),
            kept(D, COLUMNS), kept(FF_PART, D), kept(FF_PART, D), kept(1, FF_PART),
        ],
        [
            tiled_out(FF_PART), whole_out(BF16, LINE, D // LINE, FF_PART),
            whole_out(BF16, LINE, FF_PART // LINE, D), whole_out(F32, 1, FF_PART),
            whole_out(F32, D, 1), whole_out(F32, D, 1),
        ],
        [(FF_PART, D), (FF_PART, D)], 3 * FF_PART, 4,
    )


def run_attention(
    order, grad, qkv, h_attn, hidden, d_pre, cos_rows, sin_rows, segments, w_out, weights, w_down,
    vec, totals,
):
    operands = (
        *grad, qkv, h_attn, hidden, d_pre, cos_rows, sin_rows,
        segments.reshape(STEPS, 1, SLOTS), segments.reshape(GROUP, 1), w_out, weights, w_down, vec,
    )
    specs = [
        *HALVES, tiled(QKV_PART), tiled(D), tiled(FF_PART), tiled(FF_PART), tiled(128), tiled(128),
        pl.BlockSpec((1, 1, SLOTS), lambda i: (i, 0, 0)), tiled(1), kept(128, D),
        kept(D, COLUMNS), kept(FF_PART, D), kept(4, D),
    ]
    sums = [(128, D), (D, QKV_PART), (1, QKV_PART)]
    work = 2 * COLUMNS + 1024
    if totals is None:
        outs = [*halves_out(), *halves_out(), *[whole_out(F32, *shape) for shape in sums]]
        return run(attention_first_kernel, "attention", operands, specs, outs, [], work, 8)
    outs = [
        *halves_out(), *halves_out(), whole_out(BF16, 128, D),
        whole_out(BF16, LINE, D // LINE, QKV_PART), whole_out(F32, 1, QKV_PART),
        whole_out(F32, D, 1), whole_out(F32, D, 1),
    ]
    return run(
        attention_last_kernel, "attention", (order, *operands, *totals),
        [SCALARS, *specs, *[kept(*shape) for shape in sums]], outs, sums[:2], work, 8,
    )


def rotary_rows(segments):
    index = jnp.arange(SLOTS, dtype=jnp.int32)[None, :]
    start = jnp.zeros_like(segments)
    for number in range(-1, 4):
        first = jnp.min(jnp.where(segments == number, index, SLOTS), axis=1, keepdims=True)
        start = jnp.where(segments == number, first, start)
    position = (index - start).astype(F32).reshape(HELD, 1)
    lane = jnp.arange(128, dtype=jnp.int32) % HEAD_DIM
    inv_freq = 10000.0 ** (-(lane % 8).astype(F32) * 2.0 / ROTARY)
    angles = position * jnp.where(lane < ROTARY, inv_freq, 0.0)[None, :]
    sign = jnp.where(lane < ROTARY // 2, -1.0, 1.0)
    return (jnp.cos(angles), jnp.sin(angles) * sign[None, :])


def on_device_plane(
    tokens, segment_ids, cotangent, w_qkv, w_out, w_up, w_down,
    b_qkv, b_out, b_up, b_down, gain_attn, shift_attn, gain_mlp, shift_mlp,
):
    me = lax.axis_index("fsdp")
    rank, core, chip, line = me % PLANE, me % 2, (me % PLANE) // 2, me // PLANE
    rows = w_up.shape[0]

    order = jnp.stack([line, line ^ (1 + core), line ^ (2 - core), line ^ 3]).astype(jnp.int32)
    turn = jnp.arange(LINE, dtype=jnp.int32) ^ line
    place = jnp.where(core == 0, turn, 2 * (turn % 2) + turn // 2)

    vectors = (b_qkv, b_out, b_up, b_down, gain_attn, shift_attn, gain_mlp, shift_mlp)
    cuts = whole(cut_kernel, jax.ShapeDtypeStruct((PLANE, rows, COLUMNS), BF16), w_up, w_qkv)
    down_own = jnp.concatenate([w_down, w_out])
    got, tok_near, down_near = together(
        over_plane(cuts), swap_near(tokens), line_near(down_own)
    )

    got = got.reshape(PLANE * rows, COLUMNS)
    block = jnp.concatenate(
        [jnp.pad(v, (0, 128 - v.shape[0])).reshape(1, 128) for v in vectors]
        + [segment_ids.astype(BF16).reshape(4, 128), jnp.zeros((4, 128), BF16)]
    )
    block = over_groups(jnp.broadcast_to(block[None], (DEVICES, 16, 128)), None)
    tok_one = jnp.concatenate([tokens, tok_near])
    got_near, tok_far, block, tok_one = together(
        line_near(got), swap_far(tokens), block, tok_one
    )

    near = 2 + 2 * core
    far = 6 - near
    ranks = PLANE * line + jnp.stack(
        [
            rank, rank ^ near, rank ^ 1, rank ^ 1 ^ far,
            rank ^ far, rank ^ 6, rank ^ 1 ^ near, rank ^ 7,
        ]
    )
    segments = jnp.take(block[:, 8:12].reshape(DEVICES, SLOTS), ranks, axis=0).astype(jnp.int32)
    cos_rows, sin_rows = rotary_rows(segments)
    vec = block[:, :8].astype(F32)
    qkv_bias = vec[:, 0, :96].reshape(3, 2, 2, 4, HEAD_DIM)
    qkv_bias = lax.dynamic_index_in_dim(qkv_bias, chip, 3, keepdims=False)
    qkv_bias = lax.dynamic_index_in_dim(qkv_bias, core, 1, keepdims=False).reshape(1, QKV_PART)
    up_bias = vec[:, 2].reshape(LINE, PLANE, 128)
    up_bias = lax.dynamic_index_in_dim(up_bias, rank, 1, keepdims=False).reshape(1, FF_PART)
    out_bias = (vec[:, 1, :32] + vec[:, 3, :32]).reshape(1, D)
    gains = vec[:, 4:, :32].transpose(1, 0, 2).reshape(4, D)
    got_pair = jnp.stack([got, got_near])
    (
        got_far, tok_diag, tok_three, cos_rows, sin_rows, qkv_bias, up_bias, gains, out_bias, got_pair
    ) = together(
        line_far(got_pair), swap_far(tok_near), swap_core(tok_one), cos_rows, sin_rows,
        qkv_bias, up_bias, gains, out_bias, got_pair,
    )

    live_rows = (segment_ids >= 0).astype(F32)
    grad_out = cotangent.astype(F32) * live_rows[:, None]
    grad_own = grad_out.astype(BF16)
    grad_send, tok_two = together(grad_own, jnp.concatenate([tok_far, tok_diag]))
    *front_near, weights = run_front(
        place, (tok_one, tok_three), (got_pair, got_far), None, cos_rows[:GROUP],
        sin_rows[:GROUP], gains, up_bias, qkv_bias,
    )
    *front_near, weights, tok_four, grad_near, grad_far = together(
        *front_near, weights, swap_core(tok_two), swap_near(grad_send), swap_far(grad_send)
    )
    grad_one = jnp.concatenate([grad_own, grad_near])
    down_pair = jnp.stack([down_own, down_near])
    front_far = run_front(
        place, (tok_two, tok_four), None, weights, cos_rows[GROUP:], sin_rows[GROUP:], gains,
        up_bias, qkv_bias,
    )
    *front_far, down_far, grad_diag, grad_three = together(
        *front_far, line_far(down_pair), swap_far(grad_near), swap_core(grad_one)
    )

    halves = jnp.concatenate([down_pair[:, 128:], down_far[:, 128:]])
    down_pieces = (down_pair[:, :128], down_far[:, :128])

    def head_rows(first):
        return jnp.stack(
            [lax.dynamic_index_in_dim(halves, place[first + i], 0, keepdims=False) for i in (0, 1)]
        )

    grad_two = jnp.concatenate([grad_far, grad_diag])
    mine = head_rows(2 * core)
    h_attn, h_mlp, hidden, slope, qkv = front_near
    mlp_near = run_mlp(place, (grad_one, grad_three), h_mlp, hidden, slope, down_pieces, weights)
    d_pre, w_down_part, *totals, grad_four, theirs = together(
        *mlp_near, swap_core(grad_two), swap_core(head_rows(2 - 2 * core))
    )
    out_part = jnp.where(
        core == 0, jnp.stack([mine, theirs], axis=1), jnp.stack([theirs, mine], axis=1)
    ).reshape(128, D)
    far_h_attn, far_h_mlp, far_hidden, far_slope, far_qkv = front_far
    far_d_pre, dw_up, dw_down, db_up, dot_two, sum_two = run_mlp_last(
        order, (grad_two, grad_four), far_h_mlp, far_hidden, far_slope, w_down_part, weights, totals
    )

    far_outs = run_attention(
        order, (grad_two, grad_four), far_qkv, far_h_attn, far_hidden, far_d_pre,
        cos_rows[GROUP:], sin_rows[GROUP:], segments[STEPS:], out_part, weights, w_down_part,
        gains, None,
    )
    out_far, out_other, norm_far, norm_other, *totals, up_half, down_half = together(
        *far_outs, line_far(dw_up[2:]), line_far(dw_down[2:])
    )
    up_half, down_half = add_low(dw_up[:2], up_half), add_low(dw_down[:2], down_half)
    out_far = add_low(out_far, swap_core(out_other))
    norm_far = add_low(norm_far, swap_core(norm_other))
    out_far, norm_far, up_half, down_half, *totals = together(
        out_far, norm_far, up_half, down_half, *totals
    )
    near_outs = run_attention(
        order, (grad_one, grad_three), qkv, h_attn, hidden, d_pre, cos_rows[:GROUP],
        sin_rows[:GROUP], segments[:STEPS], out_part, weights, w_down_part, gains, totals,
    )
    up_rows = finish(up_half).astype(BF16).reshape(PLANE, rows, FF_PART)
    (
        out_near, out_other, norm_near, norm_other, dw_out, dw_qkv, db_qkv, dot_one, sum_one,
        out_far, norm_far, up_rows, down_half,
    ) = together(
        *near_outs, swap_far(out_far), swap_far(norm_far), up_rows, finish(down_half)
    )
    grad_w_down = down_half

    pieces = dw_out.reshape(2, 2, 32, D)
    mine = lax.dynamic_index_in_dim(pieces, core, 1, keepdims=False)
    theirs = lax.dynamic_index_in_dim(pieces, 1 - core, 1, keepdims=False)
    out_other, norm_other, theirs, qkv_half = together(
        swap_core(out_other), swap_core(norm_other), swap_core(theirs), line_far(dw_qkv[2:])
    )

    def add_three(first, second, third):
        return (first.astype(F32) + second.astype(F32) + third.astype(F32)).astype(BF16)

    norm_pair = add_three(norm_near, norm_other, norm_far)
    out_pair = add_three(out_near, out_other, out_far)
    qkv_half = add_low(dw_qkv[:2], qkv_half)

    def head_half(z):
        return jnp.where(
            z // 2 == core,
            lax.dynamic_index_in_dim(mine, z % 2, 0, keepdims=False),
            lax.dynamic_index_in_dim(theirs, z % 2, 0, keepdims=False),
        )

    pieces = jnp.stack([head_half(order[i]) for i in range(LINE)])
    norm_last, out_last, qkv_rows, pieces = together(
        swap_near(norm_pair[SLOTS:]), swap_near(out_pair[SLOTS:]), finish(qkv_half),
        add_low(pieces[:2], line_far(pieces[2:])),
    )
    qkv_rows = over_plane(qkv_rows.astype(BF16).reshape(PLANE, rows, QKV_PART))
    grad_w_qkv = whole(place_qkv_kernel, jax.ShapeDtypeStruct((rows, 3 * D), F32), qkv_rows)
    up_rows = over_plane(up_rows)
    grad_w_up = whole(place_up_kernel, jax.ShapeDtypeStruct((rows, 4 * D), F32), up_rows)
    grad_w_out = finish(pieces)
    inputs = tokens.astype(F32)
    layer_out = (
        inputs + out_pair[:SLOTS].astype(F32) + out_last.astype(F32) + out_bias
    ).astype(BF16)

    def at(index, count):
        return (jnp.arange(count) == index).astype(F32)

    db_qkv = db_qkv.reshape(3, 1, 2, 1, HEAD_DIM)
    db_qkv = db_qkv * at(core, 2)[:, None, None, None] * at(chip, 4)[:, None]
    db_up = db_up.reshape(LINE, 1, 128) * at(rank, PLANE)[:, None]
    dot_one, sum_one = dot_one.reshape(1, D), sum_one.reshape(1, D)
    dot_two, sum_two = dot_two.reshape(1, D), sum_two.reshape(1, D)
    sums = jnp.concatenate(
        [
            db_qkv.reshape(DEVICES, 96),
            column_sums(grad_own).reshape(DEVICES, 32),
            db_up.reshape(DEVICES, 128),
            ((dot_one - gains[1:2] * sum_one) / gains[0:1]).reshape(DEVICES, 32),
            sum_one.reshape(DEVICES, 32),
            ((dot_two - gains[3:4] * sum_two) / gains[2:3]).reshape(DEVICES, 32),
            sum_two.reshape(DEVICES, 32),
        ],
        axis=1,
    )
    sums = over_groups(sums.reshape(DEVICES, 3, 128), None)
    sums = jnp.sum(sums, axis=0).reshape(384)

    normed, inv_scale = normalize(inputs)
    d_norm = norm_pair[:SLOTS].astype(F32) + norm_last.astype(F32)
    d_inner = (
        d_norm
        - jnp.mean(d_norm, axis=-1, keepdims=True)
        - normed * jnp.mean(d_norm * normed, axis=-1, keepdims=True)
    )
    tokens_grad = grad_out + d_inner * inv_scale
    return (
        layer_out,
        tokens_grad,
        grad_w_qkv,
        grad_w_out,
        grad_w_up,
        grad_w_down,
        sums[:96],
        sums[96:128],
        sums[128:256],
        sums[96:128],
        sums[256:288],
        sums[288:320],
        sums[320:352],
        sums[352:384],
    )


def choose(mesh):
    return on_device_plane if mesh.shape["fsdp"] == DEVICES else on_device_any


def solution(mesh):
    in_specs = (
        P("fsdp", None),
        P("fsdp"),
        P("fsdp", None),
        P("fsdp", None),
        P("fsdp", None),
        P("fsdp", None),
        P("fsdp", None),
        P("fsdp"),
        P("fsdp"),
        P("fsdp"),
        P("fsdp"),
        P("fsdp"),
        P("fsdp"),
        P("fsdp"),
        P("fsdp"),
    )
    out_specs = (
        P("fsdp", None),
        P("fsdp", None),
        P("fsdp", None),
        P("fsdp", None),
        P("fsdp", None),
        P("fsdp", None),
        P("fsdp"),
        P("fsdp"),
        P("fsdp"),
        P("fsdp"),
        P("fsdp"),
        P("fsdp"),
        P("fsdp"),
        P("fsdp"),
    )
    return jax.shard_map(
        choose(mesh), mesh=mesh, in_specs=in_specs, out_specs=out_specs, check_vma=False
    )
```
